32 devices in a mesh: groups: 2 (over x), gx: 16 (over z, y, core).
Axes of the slice: x: 2, y: 2, z: 4, core: 2. Of those that a mesh axis runs over, the one named last changes fastest.
Arguments:
- charges: bfloat16 [64, 16384], P(None, ('groups', 'gx')), parts along dimension 1
- cells: int32 [16384], P(('groups', 'gx')), parts along dimension 0, may hold values from 0 to 4095
- counts: int32 [1024], P(('groups', 'gx')), parts along dimension 0, may hold values from 8 to 16, as said below
- bricks: int32 [1024], P(('groups', 'gx')), parts along dimension 0, may hold values from 0 to 31, as said below
- spline: bfloat16 [3, 4, 16384], P(None, None, ('groups', 'gx')), parts along dimension 2, as said below
- spectral_filter: float32 [128, 128, 128], P(None, 'gx'), as said below
Outputs:
- potential: bfloat16 [64, 16384], P(None, ('groups', 'gx')), parts along dimension 1
- mesh_potential: bfloat16 [64, 256, 128, 128], P(None, ('groups', 'gx')), parts along dimension 1
- spline_grad: float32 [3, 4, 16384], P(None, None, ('groups', 'gx')), parts along dimension 2
The draws below stay inside these ranges and needn't reach their ends.
There are 2 independent parts, one for each index of `groups`. The reference program is written for one: setup_inputs(seed, part) draws one part's arguments, and reference() takes and returns one part's arrays. A program takes and returns all parts, laid end to end along the dimension named above; an argument that names none is the same for every part. Nothing has to cross between parts.
Inputs may be any that keep to these rules, and one draw needn't show every extreme that they name: `counts`: every slab has a block whose slots are all live. Within each slab its 32 blocks name each of the slab's 32 bricks once. For each atom and dimension the four weights are the cubic B-spline weights of one fraction in [0, 1), for the mesh offsets -1, 0, 1, 2, rounded to bfloat16. `spectral_filter`: the filter has the same value at the wave numbers m and -m, indices taken modulo 128, 128, 128.
All inputs are finite; a program needn't handle non-finite values.
Results may differ from the reference program's by a relative error of at most 0.0052.
The reference program's roundings to bfloat16 on the way count: a program that leaves them out, or rounds other values in their place, can miss the bound.
Values may be sent and summed in bfloat16 or wider, within the bound.
A program may use at most 256 MiB of HBM per device.

```python
import math
import jax
import jax.numpy as jnp
from jax import lax

C = 64
NX = 128
NY = 128
NZ = 128
BY = 4
BLK = 16
CX = 8
NB = 32
ATOMS = 8192
BLOCKS = 512


def draw_charges(key, part):
    key = jax.random.fold_in(key, 11)
    key_value = jax.random.fold_in(key, 0)
    return jax.random.normal(key_value, (C, ATOMS), jnp.float32).astype(jnp.bfloat16)


def draw_counts(key, part):
    key = jax.random.fold_in(key, 21)
    key_base, key_full = jax.random.split(key)
    slab_count = BLOCKS // NB
    base_count = jax.random.randint(key_base, (slab_count, NB), BLK // 2, BLK + 1)
    full_block = jax.random.randint(key_full, (slab_count, 1), 0, NB)
    chosen = jnp.where(jnp.arange(NB, dtype=jnp.int32)[None, :] == full_block, BLK, base_count)
    return chosen.reshape(BLOCKS).astype(jnp.int32)


def draw_bricks(key, part):
    key = jax.random.fold_in(key, 22)
    slab_count = BLOCKS // NB
    scores = jax.random.randint(key, (slab_count, NB), 0, 1 << 20) * NB + jnp.arange(NB, dtype=jnp.int32)[None, :]
    return jnp.argsort(scores, axis=1).astype(jnp.int32).reshape(BLOCKS)


def draw_spline(key, part):
    key = jax.random.fold_in(key, 12)
    fraction = jax.random.uniform(key, (3, 1, ATOMS), jnp.float32)
    rest = 1.0 - fraction
    cube = fraction * fraction * fraction
    square = fraction * fraction
    first_weight = rest * rest * rest / 6.0
    second_weight = (3.0 * cube - 6.0 * square + 4.0) / 6.0
    third_weight = (-3.0 * cube + 3.0 * square + 3.0 * fraction + 1.0) / 6.0
    fourth_weight = cube / 6.0
    return jnp.concatenate([first_weight, second_weight, third_weight, fourth_weight], axis=1).astype(jnp.bfloat16)


def draw_spectral_filter(key, part):
    key = jax.random.fold_in(key, 13)
    raw_values = jax.random.uniform(key, (NX, NY, NZ), jnp.float32, 0.5, 1.5)
    mirror = jnp.roll(jnp.flip(raw_values, (0, 1, 2)), 1, (0, 1, 2))
    symmetric = 0.5 * (raw_values + mirror)
    return symmetric


def set_ends(drawn, stream_key, smallest, top_value):
    index_at = [jax.random.randint(jax.random.fold_in(stream_key, axis), (), 0, length) for axis, length in enumerate(drawn.shape)]
    widest = drawn.shape.index(max(drawn.shape))
    beside = index_at[:widest] + [(index_at[widest] + 1) % drawn.shape[widest]] + index_at[widest + 1:]
    return drawn.at[tuple(index_at)].set(smallest).at[tuple(beside)].set(top_value)


def setup_inputs(seed: int = 0, part: int = 0) -> dict:
    key_list = jax.random.split(jax.random.key(seed), 7)
    part_keys = jax.random.split(jax.random.fold_in(key_list[6], part), 7)
    return {
        "charges": draw_charges(jax.random.fold_in(jax.random.fold_in(key_list[6], part), 71), part),
        "cells": set_ends(jax.random.randint(part_keys[1], (ATOMS,), 0, CX * BY * NZ), jax.random.fold_in(part_keys[1], 1), 0, (CX * BY * NZ) - 1).astype(jnp.int32),
        "counts": draw_counts(jax.random.fold_in(jax.random.fold_in(key_list[6], part), 71), part),
        "bricks": draw_bricks(jax.random.fold_in(jax.random.fold_in(key_list[6], part), 71), part),
        "spline": draw_spline(jax.random.fold_in(jax.random.fold_in(key_list[6], part), 71), part),
        "spectral_filter": draw_spectral_filter(jax.random.fold_in(key_list[6], 71), part),
    }


SMEAR_WIDTH = 0.5


def signed_wave(length):
    index = jnp.arange(length, dtype=jnp.int32)
    signed = jnp.where(index < length // 2, index, index - length)
    return (2.0 * math.pi / length) * signed.astype(jnp.float32)


def coulomb_kernel(spectral_filter, row_offset):
    rows_y = spectral_filter.shape[1]
    wave_x = signed_wave(NX)[:, None, None]
    wave_y = lax.dynamic_slice_in_dim(signed_wave(NY), row_offset, rows_y)[None, :, None]
    wave_z = signed_wave(NZ)[None, None, :]
    squared = wave_x * wave_x + wave_y * wave_y + wave_z * wave_z
    safe_sq = jnp.where(squared > 0, squared, 1.0)
    value = 4.0 * math.pi * spectral_filter * jnp.exp(-0.5 * SMEAR_WIDTH * SMEAR_WIDTH * squared) / safe_sq
    return jnp.where(squared > 0, value, 0.0)


def rounded(complex_field):
    real_part = lax.optimization_barrier(complex_field.real.astype(jnp.bfloat16)).astype(jnp.float32)
    imag_part = lax.optimization_barrier(complex_field.imag.astype(jnp.bfloat16)).astype(jnp.float32)
    return real_part + 1j * imag_part


def reference(charges, cells, counts, bricks, spline, spectral_filter):
    slot_index = jnp.arange(ATOMS, dtype=jnp.int32)
    block_index = slot_index // BLK
    slab_index = slot_index // (BLK * NB)
    live_mask = (slot_index % BLK) < counts[block_index]
    pos_x = slab_index * CX + cells // (BY * NZ)
    pos_y = bricks[block_index] * BY + (cells // NZ) % BY
    pos_z = cells % NZ
    kept_charges = jnp.where(live_mask[None, :], charges, jnp.zeros_like(charges)).astype(jnp.float32)
    weights = jnp.where(live_mask[None, None, :], spline.astype(jnp.float32), jnp.float32(0.0))
    kept_rows = kept_charges.T

    def flat_index(offset_x, offset_y, offset_z):
        plane = (pos_x + offset_x - 1) % NX
        row = (pos_y + offset_y - 1) % NY
        column = (pos_z + offset_z - 1) % NZ
        return ((plane * NY + row) * NZ + column).astype(jnp.int32)

    density = jnp.zeros((NX * NY * NZ, C), jnp.float32)
    for offset_x in range(4):
        for offset_y in range(4):
            lifted = kept_rows * (weights[0, offset_x] * weights[1, offset_y])[:, None]
            lifted = lax.optimization_barrier(lifted.astype(jnp.bfloat16)).astype(jnp.float32)
            for offset_z in range(4):
                density = density.at[flat_index(offset_x, offset_y, offset_z)].add(lifted * weights[2, offset_z][:, None])

    pair_grid = density.reshape(NX, NY, NZ, C // 2, 2)
    kernel = coulomb_kernel(spectral_filter, jnp.int32(0))

    def one_pair(pair_index):
        pair_field = lax.dynamic_index_in_dim(pair_grid, pair_index, 3, keepdims=False)
        complex_field = pair_field[..., 0] + 1j * pair_field[..., 1]
        spectrum = jnp.fft.fft(jnp.fft.fft(complex_field, axis=2), axis=1)
        spectrum = rounded(spectrum)
        spectrum = jnp.fft.ifft(kernel * jnp.fft.fft(spectrum, axis=0), axis=0)
        spectrum = rounded(spectrum)
        spectrum = jnp.fft.ifft(jnp.fft.ifft(spectrum, axis=1), axis=2)
        return jnp.stack([spectrum.real, spectrum.imag]).astype(jnp.bfloat16)

    mesh_pairs = lax.map(one_pair, jnp.arange(C // 2, dtype=jnp.int32))
    mesh_potential = mesh_pairs.reshape(C, NX, NY, NZ)

    field_rows = mesh_potential.reshape(C, NX * NY * NZ).T
    potential = jnp.zeros((ATOMS, C), jnp.float32)
    grad_x = [jnp.zeros((ATOMS,), jnp.float32) for offset in range(4)]
    grad_y = [jnp.zeros((ATOMS,), jnp.float32) for offset in range(4)]
    grad_z = [jnp.zeros((ATOMS,), jnp.float32) for offset in range(4)]
    for offset_x in range(4):
        for offset_y in range(4):
            for offset_z in range(4):
                sampled = field_rows[flat_index(offset_x, offset_y, offset_z)].astype(jnp.float32)
                weight = weights[0, offset_x] * weights[1, offset_y] * weights[2, offset_z]
                potential = potential + weight[:, None] * sampled
                intersection = jnp.sum(sampled * kept_rows, axis=1)
                grad_x[offset_x] = grad_x[offset_x] + weights[1, offset_y] * weights[2, offset_z] * intersection
                grad_y[offset_y] = grad_y[offset_y] + weights[0, offset_x] * weights[2, offset_z] * intersection
                grad_z[offset_z] = grad_z[offset_z] + weights[0, offset_x] * weights[1, offset_y] * intersection
    spline_grad = jnp.stack([jnp.stack(grad_x), jnp.stack(grad_y), jnp.stack(grad_z)])
    return potential.T.astype(jnp.bfloat16), mesh_potential, spline_grad
```

```python
import math

import jax
import jax.numpy as jnp
from jax import lax
from jax.experimental import pallas as pl
from jax.experimental.pallas import tpu as pltpu
from jax.sharding import PartitionSpec as P

NX = 128
NY = 128
NZ = 128
BY = 4
PARTS = 2


PRECISE = lax.Precision.HIGH
SMEAR_WIDTH = 0.5


def shifted(block, axis, distance):
    devices = range(lax.axis_size(axis))
    route = [((i - distance) % len(devices), i) for i in devices]
    return lax.ppermute(block, axis, route)


def signed_wave(length):
    index = jnp.arange(length, dtype=jnp.int32)
    signed = jnp.where(index < length // 2, index, index - length)
    return 2.0 * math.pi / length * signed.astype(jnp.float32)


def coulomb_kernel(spectral_filter, row_offset):
    rows_y = spectral_filter.shape[1]
    wave_x = signed_wave(NX)[:, None, None]
    wave_y = lax.dynamic_slice_in_dim(signed_wave(NY), row_offset, rows_y)[None, :, None]
    wave_z = signed_wave(NZ)[None, None, :]
    squared = wave_x * wave_x + wave_y * wave_y + wave_z * wave_z
    safe_sq = jnp.where(squared > 0, squared, 1.0)
    value = (
        4.0
        * math.pi
        * spectral_filter
        * jnp.exp(-0.5 * SMEAR_WIDTH * SMEAR_WIDTH * squared)
        / safe_sq
    )
    return jnp.where(squared > 0, value, 0.0)


def complex_table(length, inverse):
    index = jnp.arange(length, dtype=jnp.int32)
    turn_count = index[:, None] * index[None, :] % length
    phase_angle = 2.0 * math.pi / length * turn_count.astype(jnp.float32)
    cosine = jnp.cos(phase_angle)
    sine_part = jnp.sin(phase_angle) * (1.0 if inverse else -1.0)
    table = jnp.stack(
        [jnp.stack([cosine, sine_part], axis=1), jnp.stack([-sine_part, cosine], axis=1)], axis=0
    )
    if inverse:
        table = table * (1.0 / length)
    return table


def transform(field, length, inverse, einsum_form):
    table = complex_table(length, inverse)
    return jnp.einsum(
        einsum_form,
        field.astype(jnp.float32),
        table,
        precision=PRECISE,
        preferred_element_type=jnp.float32,
    )


def packed_atoms(charges, cells, counts, spline):
    blocks = counts.shape[0]
    width = cells.shape[0] // blocks
    rank = jnp.arange(width, dtype=jnp.int32)
    live = (rank[None, :] < counts[:, None]).reshape(1, -1)
    kept_charges = jnp.where(live, charges, jnp.zeros_like(charges))
    kept_weights = jnp.where(live, spline.reshape(12, -1), jnp.zeros((), spline.dtype))
    place = jnp.stack([cells // (BY * NZ), cells // NZ % BY, cells % NZ]).astype(jnp.bfloat16)
    packed = jnp.concatenate([place, kept_weights, kept_charges], axis=0)
    return packed.reshape(packed.shape[0], blocks, width)


def by_brick(packed, bricks):
    blocks = bricks.shape[0]
    chosen = (bricks[:, None] == jnp.arange(blocks, dtype=jnp.int32)[None, :]).astype(jnp.bfloat16)
    return jnp.einsum(
        "fba,bn->fna", packed, chosen, preferred_element_type=jnp.float32
    ).astype(jnp.bfloat16)


def unpack(packed):
    place = packed[:3].astype(jnp.int32)
    weights = packed[3:15].astype(jnp.float32).reshape((3, 4) + packed.shape[1:])
    return place, weights, packed[15:]


def dense_weights(weights, start, size):
    row = jnp.arange(size, dtype=jnp.int32)[None, :, None]
    total = 0.0
    for offset in range(4):
        hit = row == start[:, None, :] + offset
        total = total + jnp.where(hit, weights[offset][:, None, :], 0.0)
    return total


def spread_tables(packed, shift_x, planes):
    place, weights, charge = unpack(packed)
    charge = charge.transpose(1, 0, 2)
    weight_x = dense_weights(weights[0], place[0] + (shift_x - 1), planes)
    weight_y = dense_weights(weights[1], place[1], BY + 3)
    column = jnp.arange(NZ, dtype=jnp.int32)[None, None, :]
    weight_z = 0.0
    for offset in range(4):
        hit = column == (place[2][:, :, None] + (offset - 1)) % NZ
        weight_z = weight_z + jnp.where(hit, weights[2, offset][:, :, None], 0.0)
    weight_z = weight_z.astype(jnp.bfloat16)

    def around(table, axis):
        return jnp.concatenate(
            [jnp.roll(table, 1, 0), table, jnp.roll(table, -1, 0)], axis=axis
        )

    none = jnp.zeros_like(weight_y)
    previous = jnp.roll(jnp.concatenate([weight_y[:, 5:7], none[:, :2]], axis=1), 1, 0)
    following = jnp.roll(jnp.concatenate([none[:, :3], weight_y[:, :1]], axis=1), -1, 0)
    rows = jnp.concatenate([previous, weight_y[:, 1:5], following], axis=2)
    pair = around(weight_x, 2)[:, :, None, :] * rows[:, None, :, :]
    pair = pair.reshape(pair.shape[0], planes * BY, pair.shape[3])
    return around(charge, 2), pair, around(weight_z, 1)


def spread_kernel(*refs):
    out_refs = refs[9:]
    planes, unused, share = out_refs[0].shape[:3]

    def part(group, first, count):
        charge = refs[3 * group][0].astype(jnp.float32)
        pair = refs[3 * group + 1][0, BY * first : BY * (first + count)]
        lifted = (charge[None] * pair[:, None, :]).astype(jnp.bfloat16)
        lifted = lifted.reshape(-1, lifted.shape[2])
        tile = jnp.dot(lifted, refs[3 * group + 2][0], preferred_element_type=jnp.float32)
        return tile.reshape((count, BY) + (charge.shape[0], NZ))

    for plane in range(planes):
        tile = part(0, plane, 1)
        if plane < 2:
            tile = tile + part(1, plane, 1)
        if plane == planes - 1:
            tile = tile + part(2, 0, 1)
        for index, out_ref in enumerate(out_refs):
            out_ref[plane : plane + 1] = tile[:, :, share * index : share * (index + 1)]


def spread(packed, bricks, planes):
    ordered = by_brick(packed, bricks)
    below = shifted(ordered, "gx", 1)
    above = shifted(ordered, "gx", -1)
    tables = [
        *spread_tables(ordered, 0, planes),
        *spread_tables(below, -planes, 2),
        *spread_tables(above, 1, 1),
    ]
    blocks = bricks.shape[0]
    share = tables[0].shape[1] // PARTS
    return pl.pallas_call(
        spread_kernel,
        grid=(blocks,),
        in_specs=[pl.BlockSpec((1,) + t.shape[1:], lambda n: (n, 0, 0)) for t in tables],
        out_specs=[pl.BlockSpec((planes, BY, share, NZ), lambda n: (0, n, 0, 0))] * PARTS,
        out_shape=[jax.ShapeDtypeStruct((planes, NY, share, NZ), jnp.float32)] * PARTS,
        compiler_params=pltpu.CompilerParams(vmem_limit_bytes=32 * 1024 * 1024),
    )(*tables)


def sample_kernel(bricks_ref, *refs):
    fields = refs[:9]
    charge_ref, column_ref, wx_ref, wy_ref, pot_ref, gx_ref, gy_ref, gz_ref = refs[9:]
    charge = charge_ref[0].astype(jnp.float32)
    wx = wx_ref[0]
    wy = wy_ref[0]
    lanes = charge.shape[1]
    hit = lax.broadcasted_iota(jnp.int32, (NZ, lanes), 0) == column_ref[0]
    hit = jnp.where(hit, 1.0, 0.0).astype(jnp.bfloat16)
    potential = jnp.zeros(charge.shape, jnp.float32)
    along_y = jnp.zeros(wy.shape, jnp.float32)
    along_z = jnp.zeros((1, lanes), jnp.float32)
    top = 0
    for group in range(3):
        before, here, after = fields[3 * group : 3 * group + 3]
        for plane in range(here.shape[0]):
            tile = jnp.concatenate(
                [before[plane, BY - 1 : BY], here[plane], after[plane, 0:2]], axis=0
            )
            rows, channels = tile.shape[:2]
            taken = jnp.dot(
                tile.reshape(rows * channels, NZ), hit, preferred_element_type=jnp.float32
            ).reshape(rows, channels, lanes)
            wx_here = wx[top : top + 1]
            weight = wx_here * wy
            potential = potential + jnp.sum(taken * weight[:, None, :], axis=0)
            dots = jnp.sum(taken * charge[None], axis=1)
            over_y = jnp.sum(dots * wy, axis=0, keepdims=True)
            gx_ref[0, top : top + 1] = over_y
            along_y = along_y + wx_here * dots
            along_z = along_z + wx_here * over_y
            top += 1
    pot_ref[0] = potential
    gy_ref[0] = along_y
    gz_ref[0] = along_z


def sample(packed, bricks, fields):
    place, weights, charge = unpack(packed)
    blocks, width = bricks.shape[0], packed.shape[2]
    channels = charge.shape[0]
    planes = sum(field.shape[0] for field in fields)
    charge_lanes = jnp.tile(charge.transpose(1, 0, 2), (1, 1, 4))
    offset = jnp.arange(4, dtype=jnp.int32)
    column = (place[2][:, None, :] + offset[None, :, None] - 1) % NZ
    column = column.reshape(blocks, 1, 4 * width)
    weight_z = weights[2].transpose(1, 0, 2)
    weight_x = jnp.tile(dense_weights(weights[0], place[0], planes), (1, 1, 4))
    weight_y = jnp.tile(dense_weights(weights[1], place[1], BY + 3), (1, 1, 4))
    lanes = 4 * width
    bricks_all = NY // BY

    def field_spec(field, step):
        return pl.BlockSpec(
            (field.shape[0], BY, channels, NZ),
            lambda n, b: (0, lax.rem(b[n] + (step + bricks_all), bricks_all), 0, 0),
        )

    def table_spec(rows):
        return pl.BlockSpec((1, rows, lanes), lambda n, b: (n, 0, 0))

    sizes = [channels, planes, BY + 3, 1]
    pot, gx, gy, gz = pl.pallas_call(
        sample_kernel,
        grid_spec=pltpu.PrefetchScalarGridSpec(
            num_scalar_prefetch=1,
            grid=(blocks,),
            in_specs=[field_spec(f, step) for f in fields for step in (-1, 0, 1)]
            + [table_spec(r) for r in (channels, 1, planes, BY + 3)],
            out_specs=[table_spec(r) for r in sizes],
        ),
        out_shape=[jax.ShapeDtypeStruct((blocks, r, lanes), jnp.float32) for r in sizes],
        compiler_params=pltpu.CompilerParams(vmem_limit_bytes=32 * 1024 * 1024),
    )(bricks, *[f for f in fields for _ in range(3)], charge_lanes, column, weight_x, weight_y)

    def split(table):
        return table.reshape(blocks, table.shape[1], 4, width)

    weight_k = weight_z[:, None]
    potential = jnp.sum(split(pot) * weight_k, axis=2)
    potential = potential.transpose(1, 0, 2).reshape(channels, -1)
    over_x = jnp.sum(split(gx) * weight_k, axis=2)
    over_y = jnp.sum(split(gy) * weight_k, axis=2)

    def pick(table, start):
        row = jnp.arange(table.shape[1], dtype=jnp.int32)[None, :, None]
        picked = [
            jnp.sum(jnp.where(row == start[:, None, :] + i, table, 0.0), axis=1) for i in range(4)
        ]
        return jnp.stack(picked)

    grad_x = pick(over_x, place[0])
    grad_y = pick(over_y, place[1])
    grad_z = split(gz)[:, 0].transpose(1, 0, 2)
    spline_grad = jnp.stack([grad_x, grad_y, grad_z]).reshape(3, 4, -1)
    return potential, spline_grad


def mesh_transform(density, spectral_filter):
    planes, rows, share, depth = density[0].shape
    devices = lax.axis_size("gx")
    planes_all, slab_rows = spectral_filter.shape[:2]
    kernel = coulomb_kernel(spectral_filter, lax.axis_index("gx") * slab_rows)
    part = share // 2
    spectra = []
    for piece in density:
        pairs = piece.reshape(planes, rows, part, 2, depth)
        field = transform(pairs, depth, False, "xyprz,rzsk->psxyk")
        field = transform(field, rows, False, "prxyz,rysk->psxkz").astype(jnp.bfloat16)
        field = field.reshape(part, 2, planes, devices, slab_rows, depth)
        spectra.append(field.transpose(3, 0, 1, 2, 4, 5))
    spectra = [lax.all_to_all(s, "gx", split_axis=0, concat_axis=0, tiled=True) for s in spectra]
    returned = []
    for spectrum in spectra:
        field = spectrum.transpose(1, 2, 0, 3, 4, 5)
        field = field.reshape(part, 2, planes_all, slab_rows, depth)
        field = transform(field, planes_all, False, "prxyz,rxsk->pskyz")
        field = transform(field * kernel[None, None], planes_all, True, "prxyz,rxsk->pskyz")
        field = field.astype(jnp.bfloat16).reshape(part, 2, devices, planes, slab_rows, depth)
        returned.append(field.transpose(2, 0, 1, 3, 4, 5))
    returned = [lax.all_to_all(s, "gx", split_axis=0, concat_axis=0, tiled=True) for s in returned]
    potentials = []
    for spectrum in returned:
        field = spectrum.transpose(1, 2, 3, 0, 4, 5).reshape(part, 2, planes, rows, depth)
        field = transform(field, rows, True, "prxyz,rysk->psxkz")
        field = transform(field, depth, True, "prxyz,rzsk->psxyk")
        potentials.append(field.reshape(2 * part, planes, rows, depth).astype(jnp.bfloat16))
    return jnp.concatenate(potentials, axis=0)


def body(charges, cells, counts, bricks, spline, spectral_filter):
    planes = NX // lax.axis_size("gx")
    packed = packed_atoms(charges, cells, counts, spline)
    density = spread(packed, bricks, planes)
    mesh_potential = mesh_transform(density, spectral_filter)
    top_plane = mesh_potential[:, planes - 1 : planes].transpose(1, 2, 0, 3)
    low_planes = mesh_potential[:, 0:2].transpose(1, 2, 0, 3)
    below_plane = shifted(top_plane, "gx", 1)
    above_planes = shifted(low_planes, "gx", -1)
    fields = [below_plane, mesh_potential.transpose(1, 2, 0, 3), above_planes]
    potential, spline_grad = sample(packed, bricks, fields)
    return (potential.astype(jnp.bfloat16), mesh_potential, spline_grad)


def solution(mesh):
    return jax.shard_map(
        body,
        mesh=mesh,
        in_specs=(
            P(None, ("groups", "gx")),
            P(("groups", "gx")),
            P(("groups", "gx")),
            P(("groups", "gx")),
            P(None, None, ("groups", "gx")),
            P(None, "gx", None),
        ),
        out_specs=(
            P(None, ("groups", "gx")),
            P(None, ("groups", "gx"), None, None),
            P(None, None, ("groups", "gx")),
        ),
        check_vma=False,
    )
```
